32 devices in a mesh: groups: 2 (over y), outer: 4 (over z), inner: 4 (over x, core).
Axes of the slice: x: 2, y: 2, z: 4, core: 2. Of those that a mesh axis runs over, the one named last changes fastest.
Arguments:
- initial_state: float32 [768], P('groups'), parts along dimension 0, may hold values from -6 to 6
- duty_codes: int32 [256], P(('groups', 'outer', 'inner')), parts along dimension 0, may hold values from 0 to 15
- dwell_counts: int32 [256], P(('groups', 'outer', 'inner')), parts along dimension 0, may hold values from 1 to 8
- coupling: float32 [2, 384, 384], replicated, as said below
- decay_rates: float32 [384], replicated, may hold values from 1e-05 to 0.03
- drive_on: float32 [384], replicated, may hold values from -0.02 to 0.02
- drive_off: float32 [384], replicated, may hold values from -0.02 to 0.02
Outputs:
- end_states: float32 [256, 384], P(('groups', 'outer', 'inner')), parts along dimension 0
The draws below stay inside these ranges and needn't reach their ends.
There are 2 independent parts, one for each index of `groups`. The reference program is written for one: setup_inputs(seed, part) draws one part's arguments, and reference() takes and returns one part's arrays. A program takes and returns all parts, laid end to end along the dimension named above; an argument that names none is the same for every part. Nothing has to cross between parts.
Inputs may be any that keep to these rules, and one draw needn't show every extreme that they name: coupling[0] and coupling[1] are each antisymmetric (the transpose of coupling[k] is minus coupling[k]); every entry lies within plus or minus 0.068 / sqrt(768), and that bound is reached.
All inputs are finite; a program needn't handle non-finite values.
Results may differ from the reference program's by a relative error of at most 0.00026.
Values sent between devices are 32-bit elements; how exact they have to be, the bound alone decides.
A program may use at most 128 MiB of HBM per device.

```python
import math
import jax
import jax.numpy as jnp
from jax import lax

M = 384
DUTY_LEVELS = 16
DWELL_MAX = 8
INTERVALS = 128


def draw_coupling(key, part):
    raw = jnp.clip(jax.random.normal(key, (2, M, M), jnp.float32), -1.7, 1.7)
    raw = raw.at[:, 0, 1].set(1.7)
    raw = raw.at[:, 1, 0].set(-1.7)
    return 0.02 * (raw - jnp.swapaxes(raw, 1, 2)) / (2.0 * M) ** 0.5


def touch_ends(entries, stream_key, least, top_value):
    longest = entries.shape.index(max(entries.shape))
    spots = []
    for shift in (0, 1):
        where = [jax.random.randint(jax.random.fold_in(stream_key, axis), (), 0, length) for axis, length in enumerate(entries.shape)]
        where[longest] = (where[longest] + shift) % entries.shape[longest]
        spots.append(tuple(where))
    return entries.at[spots[0]].set(least).at[spots[1]].set(top_value)


def noise(rng, extent, deviation, bound, kind=jnp.bfloat16):
    return jnp.clip(deviation * jax.random.normal(rng, extent, jnp.float32), -bound, bound).astype(kind)


def setup_inputs(seed: int = 0, part: int = 0) -> dict:
    keys = jax.random.split(jax.random.key(seed), 8)
    part_splits = jax.random.split(jax.random.fold_in(keys[7], part), 8)
    return {
        "initial_state": noise(part_splits[0], (M,), 1.0, 6.0, jnp.float32),
        "duty_codes": touch_ends(jax.random.randint(part_splits[1], (INTERVALS,), 0, DUTY_LEVELS), jax.random.fold_in(part_splits[1], 1), 0, DUTY_LEVELS - 1).astype(jnp.int32),
        "dwell_counts": touch_ends(jax.random.randint(part_splits[2], (INTERVALS,), 1, DWELL_MAX + 1), jax.random.fold_in(part_splits[2], 1), 1, DWELL_MAX).astype(jnp.int32),
        "coupling": draw_coupling(jax.random.fold_in(keys[7], 71), part),
        "decay_rates": jnp.clip(jnp.exp(jax.random.uniform(keys[4], (M,), jnp.float32, math.log(9.999999747378752e-06), math.log(0.03))), 9.999999747378752e-06, 0.03),
        "drive_on": noise(keys[5], (M,), 0.003, 0.02, jnp.float32),
        "drive_off": noise(keys[6], (M,), 0.003, 0.02, jnp.float32),
    }


def interval_step(state, codes, coupling, decay_rates, drive_on, drive_off, identity):
    duty, dwell = codes
    frac = (duty.astype(jnp.float32) + 0.5) / DUTY_LEVELS
    counts = dwell.astype(jnp.float32)
    keep = jnp.exp(-counts * decay_rates)
    mixing = identity + frac * coupling[0] + (1.0 - frac) * coupling[1]
    matrix = keep[:, None] * mixing
    offset = (counts / DWELL_MAX) * (frac * drive_on + (1.0 - frac) * drive_off)
    nxt = jnp.dot(matrix, state, precision=lax.Precision.HIGHEST) + offset
    return nxt, nxt


def reference(initial_state, duty_codes, dwell_counts, coupling, decay_rates, drive_on, drive_off):
    identity = jnp.eye(M, dtype=jnp.float32)

    def advance(state, codes):
        return interval_step(state, codes, coupling, decay_rates, drive_on, drive_off, identity)

    final, states = lax.scan(advance, initial_state, (duty_codes, dwell_counts))
    return states
```

```python
import functools
import jax
import jax.numpy as jnp
from jax import lax
from jax.experimental import pallas as pl
from jax.experimental.pallas import tpu as pltpu
from jax.sharding import PartitionSpec as P

DUTY_LEVELS = 16
DWELL_MAX = 8
LANES = 128
SUB = 8


def replay(axes, local, codes, x0, coupling, decay_col, decay_row, on_col, on_row, off_col, off_row,
           out, plus, minus, keep_col, keep_row, drive_col, drive_row):
    width = x0.shape[1]
    blocks = width // LANES
    me = lax.axis_index(axes)
    row_id = lax.broadcasted_iota(jnp.int32, (width, width), 0)
    col_id = lax.broadcasted_iota(jnp.int32, (width, width), 1)

    def tabulate_duty(level, unused):
        frac = (level.astype(jnp.float32) + 0.5) / DUTY_LEVELS
        mixing = frac * coupling[0] + (1.0 - frac) * coupling[1]
        eye = jnp.where(row_id == col_id, 1.0, 0.0).astype(jnp.float32)
        plus[level] = eye + mixing
        minus[level] = eye - mixing
        drive_col[level] = jnp.broadcast_to(frac * on_col[...] + (1.0 - frac) * off_col[...], (width, LANES))
        drive_row[level] = jnp.broadcast_to(frac * on_row[...] + (1.0 - frac) * off_row[...], (SUB, width))
        return 0

    lax.fori_loop(0, DUTY_LEVELS, tabulate_duty, 0)

    def tabulate_dwell(level, unused):
        count = level.astype(jnp.float32) + 1.0
        keep_col[level] = jnp.broadcast_to(jnp.exp(-count * decay_col[...]), (width, LANES))
        keep_row[level] = jnp.broadcast_to(jnp.exp(-count * decay_row[...]), (SUB, width))
        return 0

    lax.fori_loop(0, DWELL_MAX, tabulate_dwell, 0)
    diag = (lax.broadcasted_iota(jnp.int32, (LANES, LANES), 0)
            == lax.broadcasted_iota(jnp.int32, (LANES, LANES), 1))

    def two_steps(first, state, place):
        duty_a, duty_b = codes[0, first], codes[0, first + 1]
        dwell_a, dwell_b = codes[1, first], codes[1, first + 1]
        scale_a = dwell_a.astype(jnp.float32) / DWELL_MAX
        scale_b = dwell_b.astype(jnp.float32) / DWELL_MAX
        parts = [state[:, LANES * k:LANES * (k + 1)] for k in range(blocks)]
        sums = [[None, None] for k in range(blocks)]
        columns = []
        for r in range(width // SUB):
            rows = slice(SUB * r, SUB * (r + 1))
            term = plus[duty_a, rows, 0:LANES] * parts[0]
            for k in range(1, blocks):
                term = term + plus[duty_a, rows, LANES * k:LANES * (k + 1)] * parts[k]
            total = jnp.sum(term, axis=1, keepdims=True)
            middle = keep_col[dwell_a - 1, rows] * total + scale_a * drive_col[duty_a, rows]
            if place is not None:
                columns.append(middle)
            for k in range(blocks):
                term = minus[duty_b, rows, LANES * k:LANES * (k + 1)] * middle
                sums[k][r % 2] = term if sums[k][r % 2] is None else sums[k][r % 2] + term
        flat = jnp.concatenate([jnp.sum(s[0] + s[1], axis=0, keepdims=True) for s in sums], axis=1)
        after = keep_row[dwell_b - 1] * jnp.broadcast_to(flat, (SUB, width)) + scale_b * drive_row[duty_b]
        if place is not None:
            per = LANES // SUB
            for k in range(blocks):
                square = jnp.concatenate(columns[per * k:per * (k + 1)], axis=0)
                out[place:place + 1, LANES * k:LANES * (k + 1)] = jnp.sum(
                    jnp.where(diag, square, 0.0), axis=0, keepdims=True)
            out[place + 1:place + 2, :] = after[0:1]
        return after

    state = jnp.broadcast_to(x0[...], (SUB, width))
    state = lax.fori_loop(0, me * (local // 2), lambda pair, state: two_steps(2 * pair, state, None), state)
    for step in range(0, local, 2):
        state = two_steps(me * local + step, state, step)


def on_device(initial_state, duty_codes, dwell_counts, coupling, decay_rates, drive_on, drive_off):
    width, local = initial_state.shape[0], duty_codes.shape[0]
    axes = ("outer", "inner")
    codes = lax.all_gather(jnp.stack([duty_codes, dwell_counts]), axes, axis=1, tiled=True)
    scratch = [
        pltpu.VMEM((DUTY_LEVELS, width, width), jnp.float32),
        pltpu.VMEM((DUTY_LEVELS, width, width), jnp.float32),
        pltpu.VMEM((DWELL_MAX, width, LANES), jnp.float32),
        pltpu.VMEM((DWELL_MAX, SUB, width), jnp.float32),
        pltpu.VMEM((DUTY_LEVELS, width, LANES), jnp.float32),
        pltpu.VMEM((DUTY_LEVELS, SUB, width), jnp.float32),
    ]
    return pl.pallas_call(
        functools.partial(replay, axes, local),
        out_shape=jax.ShapeDtypeStruct((local, width), jnp.float32),
        in_specs=[pl.BlockSpec(memory_space=pltpu.SMEM)] + [pl.BlockSpec(memory_space=pltpu.VMEM)] * 8,
        out_specs=pl.BlockSpec(memory_space=pltpu.VMEM),
        scratch_shapes=scratch,
        compiler_params=pltpu.CompilerParams(vmem_limit_bytes=48 * 2**20),
    )(codes, initial_state[None, :], coupling, decay_rates[:, None], decay_rates[None, :],
      drive_on[:, None], drive_on[None, :], drive_off[:, None], drive_off[None, :])


def solution(mesh):
    return jax.shard_map(
        on_device,
        mesh=mesh,
        in_specs=(
            P("groups"),
            P(("groups", "outer", "inner")),
            P(("groups", "outer", "inner")),
            P(),
            P(),
            P(),
            P(),
        ),
        out_specs=P(("groups", "outer", "inner"), None),
        check_vma=False,
    )
```

```python
import functools
import jax
import jax.numpy as jnp
from jax import lax
from jax.experimental import pallas as pl
from jax.experimental.pallas import tpu as pltpu
from jax.sharding import PartitionSpec as P

DUTY_LEVELS = 16
DWELL_MAX = 8
LANES = 128
SUB = 8


def replay(axes, local, duty, dwell, x0, coupling_hbm, decay, on, off, out,
           plus, minus, keep_col, keep_row, drive_col, drive_row, coupling, packed, landed, codes,
           send_sem, recv_sem, coupling_sem, codes_sem):
    width = x0.shape[0]
    blocks = width // LANES
    inner = lax.axis_size(axes[1])
    count = lax.axis_size(axes[0]) * inner
    me = lax.axis_index(axes)

    def place_of(index):
        return {axes[0]: index // inner, axes[1]: index % inner}

    def push(target):
        return pltpu.make_async_remote_copy(
            src_ref=packed, dst_ref=landed.at[me], send_sem=send_sem.at[target], recv_sem=recv_sem.at[me],
            device_id=place_of(target), device_id_type=pl.DeviceIdType.MESH)

    barrier = pltpu.get_barrier_semaphore()

    def greet(source, unused):
        pl.semaphore_signal(barrier, inc=1, device_id=place_of(source), device_id_type=pl.DeviceIdType.MESH)
        return 0

    lax.fori_loop(0, me, greet, 0)
    load = pltpu.make_async_copy(coupling_hbm, coupling, coupling_sem)
    load.start()
    lane = lax.broadcasted_iota(jnp.int32, (1, LANES), 1)
    line = jnp.zeros((1, LANES), jnp.int32)
    for step in range(local):
        line = jnp.where(lane == step, duty[step], line)
        line = jnp.where(lane == local + step, dwell[step], line)
    packed[...] = line
    landed[me] = line

    @pl.when(me < count - 1)
    def to_later():
        pl.semaphore_wait(barrier, count - 1 - me)

        def send(target, unused):
            push(target).start()
            return 0

        lax.fori_loop(me + 1, count, send, 0)

    load.wait()
    diag = (lax.broadcasted_iota(jnp.int32, (LANES, LANES), 0)
            == lax.broadcasted_iota(jnp.int32, (LANES, LANES), 1))

    def columns_of(row):
        return jnp.concatenate([
            jnp.sum(jnp.where(diag, row[:, LANES * k:LANES * (k + 1)], 0.0), axis=1, keepdims=True)
            for k in range(blocks)], axis=0)

    decay_row, on_row, off_row = (ref[...].reshape(1, width) for ref in (decay, on, off))
    decay_col, on_col, off_col = (columns_of(row) for row in (decay_row, on_row, off_row))
    row_id = lax.broadcasted_iota(jnp.int32, (width, width), 0)
    col_id = lax.broadcasted_iota(jnp.int32, (width, width), 1)

    def tabulate_duty(level, unused):
        frac = (level.astype(jnp.float32) + 0.5) / DUTY_LEVELS
        mixing = frac * coupling[0] + (1.0 - frac) * coupling[1]
        eye = jnp.where(row_id == col_id, 1.0, 0.0).astype(jnp.float32)
        plus[level] = eye + mixing
        minus[level] = eye - mixing
        drive_col[level] = jnp.broadcast_to(frac * on_col + (1.0 - frac) * off_col, (width, LANES))
        drive_row[level] = jnp.broadcast_to(frac * on_row + (1.0 - frac) * off_row, (SUB, width))
        return 0

    lax.fori_loop(0, DUTY_LEVELS, tabulate_duty, 0)

    def tabulate_dwell(level, unused):
        steps = level.astype(jnp.float32)
        keep_col[level] = jnp.broadcast_to(jnp.exp(-steps * decay_col), (width, LANES))
        keep_row[level] = jnp.broadcast_to(jnp.exp(-steps * decay_row), (SUB, width))
        return 0

    lax.fori_loop(0, DWELL_MAX + 1, tabulate_dwell, 0)

    def receive(source, unused):
        pltpu.make_async_remote_copy(
            src_ref=packed, dst_ref=landed.at[source], send_sem=send_sem.at[me], recv_sem=recv_sem.at[source],
            device_id=place_of(source), device_id_type=pl.DeviceIdType.MESH).wait_recv()
        return 0

    lax.fori_loop(0, me, receive, 0)
    unload = pltpu.make_async_copy(landed, codes, codes_sem)
    unload.start()
    unload.wait()

    def two_steps(owner, first, state, place):
        duty_a, duty_b = codes[owner, 0, first], codes[owner, 0, first + 1]
        dwell_a, dwell_b = codes[owner, 0, local + first], codes[owner, 0, local + first + 1]
        scale_a = dwell_a.astype(jnp.float32) / DWELL_MAX
        scale_b = dwell_b.astype(jnp.float32) / DWELL_MAX
        parts = [state[:, LANES * k:LANES * (k + 1)] for k in range(blocks)]
        sums = [[None, None] for k in range(blocks)]
        columns = []
        for r in range(width // SUB):
            rows = slice(SUB * r, SUB * (r + 1))
            term = plus[duty_a, rows, 0:LANES] * parts[0]
            for k in range(1, blocks):
                term = term + plus[duty_a, rows, LANES * k:LANES * (k + 1)] * parts[k]
            total = jnp.sum(term, axis=1, keepdims=True)
            middle = keep_col[dwell_a, rows] * total + scale_a * drive_col[duty_a, rows]
            if place is not None:
                columns.append(middle)
            for k in range(blocks):
                term = minus[duty_b, rows, LANES * k:LANES * (k + 1)] * middle
                sums[k][r % 2] = term if sums[k][r % 2] is None else sums[k][r % 2] + term
        flat = jnp.concatenate([jnp.sum(s[0] + s[1], axis=0, keepdims=True) for s in sums], axis=1)
        after = keep_row[dwell_b] * jnp.broadcast_to(flat, (SUB, width)) + scale_b * drive_row[duty_b]
        if place is not None:
            per = LANES // SUB
            for k in range(blocks):
                square = jnp.concatenate(columns[per * k:per * (k + 1)], axis=0)
                out[place:place + 1, LANES * k:LANES * (k + 1)] = jnp.sum(
                    jnp.where(diag, square, 0.0), axis=0, keepdims=True)
            out[place + 1:place + 2, :] = after[0:1]
        return after

    half = local // 2
    state = jnp.broadcast_to(x0[...].reshape(1, width), (SUB, width))
    state = lax.fori_loop(
        0, me * half, lambda pair, state: two_steps(pair // half, 2 * (pair % half), state, None), state)
    for step in range(0, local, 2):
        state = two_steps(me, step, state, step)

    def finish(target, unused):
        push(target).wait_send()
        return 0

    lax.fori_loop(me + 1, count, finish, 0)


def on_device(initial_state, duty_codes, dwell_counts, coupling, decay_rates, drive_on, drive_off):
    width, local = initial_state.shape[0], duty_codes.shape[0]
    axes = ("outer", "inner")
    count = lax.axis_size(axes[0]) * lax.axis_size(axes[1])
    scratch = [
        pltpu.VMEM((DUTY_LEVELS, width, width), jnp.float32),
        pltpu.VMEM((DUTY_LEVELS, width, width), jnp.float32),
        pltpu.VMEM((DWELL_MAX + 1, width, LANES), jnp.float32),
        pltpu.VMEM((DWELL_MAX + 1, SUB, width), jnp.float32),
        pltpu.VMEM((DUTY_LEVELS, width, LANES), jnp.float32),
        pltpu.VMEM((DUTY_LEVELS, SUB, width), jnp.float32),
        pltpu.VMEM(coupling.shape, jnp.float32),
        pltpu.VMEM((1, LANES), jnp.int32),
        pltpu.VMEM((count, 1, LANES), jnp.int32),
        pltpu.SMEM((count, 1, LANES), jnp.int32),
        pltpu.SemaphoreType.DMA((count,)),
        pltpu.SemaphoreType.DMA((count,)),
        pltpu.SemaphoreType.DMA,
        pltpu.SemaphoreType.DMA,
    ]
    smem, vmem = pl.BlockSpec(memory_space=pltpu.SMEM), pl.BlockSpec(memory_space=pltpu.VMEM)
    return pl.pallas_call(
        functools.partial(replay, axes, local),
        out_shape=jax.ShapeDtypeStruct((local, width), jnp.float32),
        in_specs=[smem, smem, vmem, pl.BlockSpec(memory_space=pl.ANY), vmem, vmem, vmem],
        out_specs=vmem,
        scratch_shapes=scratch,
        compiler_params=pltpu.CompilerParams(
            vmem_limit_bytes=56 * 2**20, collective_id=0, has_side_effects=True),
    )(duty_codes, dwell_counts, initial_state, coupling, decay_rates, drive_on, drive_off)


def solution(mesh):
    return jax.shard_map(
        on_device,
        mesh=mesh,
        in_specs=(
            P("groups"),
            P(("groups", "outer", "inner")),
            P(("groups", "outer", "inner")),
            P(),
            P(),
            P(),
            P(),
        ),
        out_specs=P(("groups", "outer", "inner"), None),
        check_vma=False,
    )
```

```python
import functools
import jax
import jax.numpy as jnp
from jax import lax
from jax.experimental import pallas as pl
from jax.experimental.pallas import tpu as pltpu
from jax.sharding import PartitionSpec as P

DUTY_LEVELS = 16
DWELL_MAX = 8
LANES = 128
SUB = 8


def replay(axes, local, duty, dwell, x0, coupling_hbm, decay, on, off, out,
           drive_out, plus, turned, keep_col, keep_row, drive_row, mixed_on, mixed_off, coupling, packed, landed,
           codes, send_sem, recv_sem, coupling_sem, codes_sem):
    width = x0.shape[0]
    blocks = width // LANES
    inner = lax.axis_size(axes[1])
    count = lax.axis_size(axes[0]) * inner
    me = lax.axis_index(axes)

    def place_of(index):
        return {axes[0]: index // inner, axes[1]: index % inner}

    def push(target):
        return pltpu.make_async_remote_copy(
            src_ref=packed, dst_ref=landed.at[me], send_sem=send_sem.at[target], recv_sem=recv_sem.at[me],
            device_id=place_of(target), device_id_type=pl.DeviceIdType.MESH)

    barrier = pltpu.get_barrier_semaphore()

    def greet(source, unused):
        pl.semaphore_signal(barrier, inc=1, device_id=place_of(source), device_id_type=pl.DeviceIdType.MESH)
        return 0

    lax.fori_loop(0, me, greet, 0)
    load = pltpu.make_async_copy(coupling_hbm, coupling, coupling_sem)
    load.start()
    lane = lax.broadcasted_iota(jnp.int32, (1, LANES), 1)
    line = jnp.zeros((1, LANES), jnp.int32)
    for step in range(local):
        line = jnp.where(lane == step, duty[step], line)
        line = jnp.where(lane == local + step, dwell[step], line)
    packed[...] = line
    landed[me] = line

    @pl.when(me < count - 1)
    def to_later():
        pl.semaphore_wait(barrier, count - 1 - me)

        def send(target, unused):
            push(target).start()
            return 0

        lax.fori_loop(me + 1, count, send, 0)

    diag = (lax.broadcasted_iota(jnp.int32, (LANES, LANES), 0)
            == lax.broadcasted_iota(jnp.int32, (LANES, LANES), 1))
    per = LANES // SUB
    tiles = [slice(LANES * k, LANES * (k + 1)) for k in range(blocks)]
    groups = [slice(SUB * r, SUB * (r + 1)) for r in range(width // SUB)]

    def column(row, k):
        return jnp.sum(jnp.where(diag, row[:, tiles[k]], 0.0), axis=1, keepdims=True)

    decay_row, on_row, off_row = (ref[...].reshape(1, width) for ref in (decay, on, off))
    for level in range(DWELL_MAX + 1):
        keep_row[level] = jnp.broadcast_to(jnp.exp(-float(level) * decay_row), (SUB, width))
    for k in range(blocks):
        rates = column(decay_row, k)
        for level in range(DWELL_MAX + 1):
            keep_col[level, tiles[k]] = jnp.broadcast_to(jnp.exp(-float(level) * rates), (LANES, LANES))
    load.wait()

    totals = [[[None] * blocks for side in range(2)] for source in range(2)]
    for k in range(blocks):
        sources = (column(on_row, k), column(off_row, k))
        for side in range(2):
            for q in range(blocks):
                square = coupling[side, tiles[k], tiles[q]]
                for source in range(2):
                    folded = jnp.sum((square * sources[source]).reshape(per, SUB, LANES), axis=0)
                    old = totals[source][side][q]
                    totals[source][side][q] = folded if old is None else old + folded

    def through(source, side):
        return -jnp.concatenate([jnp.sum(t, axis=0, keepdims=True) for t in totals[source][side]], axis=1)

    through_on = [through(0, side) for side in range(2)]
    through_off = [through(1, side) for side in range(2)]

    def tabulate_duty(level, unused):
        frac = (level.astype(jnp.float32) + 0.5) / DUTY_LEVELS
        for k in range(blocks):
            for q in range(blocks):
                mixing = frac * coupling[0, tiles[k], tiles[q]] + (1.0 - frac) * coupling[1, tiles[k], tiles[q]]
                if k == q:
                    eye = jnp.where(diag, 1.0, 0.0)
                    plus[level, tiles[k], tiles[q]] = eye + mixing
                    turned[level, tiles[k]] = mixing - eye
                else:
                    plus[level, tiles[k], tiles[q]] = mixing
        drive_row[level] = jnp.broadcast_to(frac * on_row + (1.0 - frac) * off_row, (SUB, width))
        mixed_on[level] = jnp.broadcast_to(
            on_row + frac * through_on[0] + (1.0 - frac) * through_on[1], (SUB, width))
        mixed_off[level] = jnp.broadcast_to(
            off_row + frac * through_off[0] + (1.0 - frac) * through_off[1], (SUB, width))
        return 0

    lax.fori_loop(0, DUTY_LEVELS, tabulate_duty, 0)

    def unload(owner):
        return pltpu.make_async_copy(landed.at[owner], codes.at[owner], codes_sem.at[owner])

    def receive(source):
        @pl.when(source < me)
        def arrive():
            pltpu.make_async_remote_copy(
                src_ref=packed, dst_ref=landed.at[source], send_sem=send_sem.at[me], recv_sem=recv_sem.at[source],
                device_id=place_of(source), device_id_type=pl.DeviceIdType.MESH).wait_recv()

    def two_steps(owner, first, state, kept=None):
        duty_a, duty_b = codes[owner, 0, first], codes[owner, 0, first + 1]
        dwell_a, dwell_b = codes[owner, 0, local + first], codes[owner, 0, local + first + 1]
        frac_a = (duty_a.astype(jnp.float32) + 0.5) / DUTY_LEVELS
        scale_a = dwell_a.astype(jnp.float32) / DWELL_MAX
        scale_b = dwell_b.astype(jnp.float32) / DWELL_MAX
        sums = [[None, None] for k in range(blocks)]
        columns = []
        for r, rows in enumerate(groups):
            term = plus[duty_a, rows, tiles[0]] * state[:, tiles[0]]
            for k in range(1, blocks):
                term = term + plus[duty_a, rows, tiles[k]] * state[:, tiles[k]]
            middle = keep_col[dwell_a, rows] * jnp.sum(term, axis=1, keepdims=True)
            if kept is not None:
                columns.append(middle)
            for k in range(blocks):
                if k == r // per:
                    term = turned[duty_b, rows] * middle
                else:
                    term = plus[duty_b, rows, tiles[k]] * middle
                sums[k][r % 2] = term if sums[k][r % 2] is None else sums[k][r % 2] + term
        flat = jnp.concatenate([jnp.sum(s[0] + s[1], axis=0, keepdims=True) for s in sums], axis=1)
        driven = scale_a * (frac_a * mixed_on[duty_b] + (1.0 - frac_a) * mixed_off[duty_b])
        after = keep_row[dwell_b] * (driven - jnp.broadcast_to(flat, (SUB, width)))
        push_b = scale_b * drive_row[duty_b]
        if kept is None:
            return after + push_b
        row = lax.broadcasted_iota(jnp.int32, (local, width), 0)
        flat = jnp.concatenate([
            jnp.sum(jnp.where(diag, jnp.concatenate(columns[per * k:per * (k + 1)], axis=0), 0.0),
                    axis=0, keepdims=True) for k in range(blocks)], axis=1)
        states = jnp.where(row == first, flat, jnp.where(row == first + 1, after[0:1], kept[0]))
        drives = jnp.where(row == first, scale_a * drive_row[duty_a, 0:1],
                           jnp.where(row == first + 1, push_b[0:1], kept[1]))
        return after + push_b, (states, drives)

    half = local // 2
    state = jnp.broadcast_to(x0[...].reshape(1, width), (SUB, width))
    receive(0)
    unload(0).start()

    def block(owner, state):
        receive(owner + 1)
        unload(owner + 1).start()
        unload(owner).wait()
        return lax.fori_loop(0, half, lambda pair, state: two_steps(owner, 2 * pair, state), state)

    state = lax.fori_loop(0, me, block, state)
    unload(me).wait()
    blank = jnp.zeros((local, width), jnp.float32)
    state, kept = lax.fori_loop(
        0, half, lambda pair, carry: two_steps(me, 2 * pair, *carry), (state, (blank, blank)))
    out[...], drive_out[...] = kept

    def finish(target, unused):
        push(target).wait_send()
        return 0

    lax.fori_loop(me + 1, count, finish, 0)


def on_device(initial_state, duty_codes, dwell_counts, coupling, decay_rates, drive_on, drive_off):
    width, local = initial_state.shape[0], duty_codes.shape[0]
    axes = ("outer", "inner")
    count = lax.axis_size(axes[0]) * lax.axis_size(axes[1])
    scratch = [
        pltpu.VMEM((DUTY_LEVELS, width, width), jnp.float32),
        pltpu.VMEM((DUTY_LEVELS, width, LANES), jnp.float32),
        pltpu.VMEM((DWELL_MAX + 1, width, LANES), jnp.float32),
        pltpu.VMEM((DWELL_MAX + 1, SUB, width), jnp.float32),
        pltpu.VMEM((DUTY_LEVELS, SUB, width), jnp.float32),
        pltpu.VMEM((DUTY_LEVELS, SUB, width), jnp.float32),
        pltpu.VMEM((DUTY_LEVELS, SUB, width), jnp.float32),
        pltpu.VMEM(coupling.shape, jnp.float32),
        pltpu.VMEM((1, LANES), jnp.int32),
        pltpu.VMEM((count, 1, LANES), jnp.int32),
        pltpu.SMEM((count, 1, LANES), jnp.int32),
        pltpu.SemaphoreType.DMA((count,)),
        pltpu.SemaphoreType.DMA((count,)),
        pltpu.SemaphoreType.DMA,
        pltpu.SemaphoreType.DMA((count,)),
    ]
    smem, vmem = pl.BlockSpec(memory_space=pltpu.SMEM), pl.BlockSpec(memory_space=pltpu.VMEM)
    states, drives = pl.pallas_call(
        functools.partial(replay, axes, local),
        out_shape=[jax.ShapeDtypeStruct((local, width), jnp.float32)] * 2,
        in_specs=[smem, smem, vmem, pl.BlockSpec(memory_space=pl.ANY), vmem, vmem, vmem],
        out_specs=[vmem, vmem],
        scratch_shapes=scratch,
        compiler_params=pltpu.CompilerParams(
            vmem_limit_bytes=56 * 2**20, collective_id=0, has_side_effects=True),
    )(duty_codes, dwell_counts, initial_state, coupling, decay_rates, drive_on, drive_off)
    return states + drives


def solution(mesh):
    return jax.shard_map(
        on_device,
        mesh=mesh,
        in_specs=(
            P("groups"),
            P(("groups", "outer", "inner")),
            P(("groups", "outer", "inner")),
            P(),
            P(),
            P(),
            P(),
        ),
        out_specs=P(("groups", "outer", "inner"), None),
        check_vma=False,
    )
```

```python
import functools
import jax
import jax.numpy as jnp
from jax import lax
from jax.experimental import pallas as pl
from jax.experimental.pallas import tpu as pltpu
from jax.sharding import PartitionSpec as P

DUTY_LEVELS = 16
DWELL_MAX = 8
LANES = 128
SUB = 8


def replay(axes, local, duty_hbm, dwell_hbm, x0_hbm, coupling_hbm, decay_hbm, on_hbm, off_hbm, out,
           drive_out, plus, turned, keep_col, keep_row, drive_row, mixed_on, mixed_off, coupling, packed, landed,
           codes, send_sem, recv_sem, coupling_sem, codes_sem, duty, dwell, x0, decay, on, off, small_sem):
    width = x0.shape[0]
    blocks = width // LANES
    inner = lax.axis_size(axes[1])
    count = lax.axis_size(axes[0]) * inner
    me = lax.axis_index(axes)

    def place_of(index):
        return {axes[0]: index // inner, axes[1]: index % inner}

    def push(target):
        return pltpu.make_async_remote_copy(
            src_ref=packed, dst_ref=landed.at[me], send_sem=send_sem.at[target], recv_sem=recv_sem.at[me],
            device_id=place_of(target), device_id_type=pl.DeviceIdType.MESH)

    barrier = pltpu.get_barrier_semaphore()

    def greet(source, unused):
        pl.semaphore_signal(barrier, inc=1, device_id=place_of(source), device_id_type=pl.DeviceIdType.MESH)
        return 0

    lax.fori_loop(0, me, greet, 0)
    load = pltpu.make_async_copy(coupling_hbm, coupling, coupling_sem)
    pairs = ((duty_hbm, duty), (dwell_hbm, dwell), (decay_hbm, decay), (on_hbm, on), (off_hbm, off), (x0_hbm, x0))
    loads = [pltpu.make_async_copy(a, b, small_sem.at[i]) for i, (a, b) in enumerate(pairs)]
    for copy in loads:
        copy.start()
    load.start()
    for copy in loads[:2]:
        copy.wait()
    lane = lax.broadcasted_iota(jnp.int32, (1, LANES), 1)
    line = jnp.zeros((1, LANES), jnp.int32)
    for step in range(local):
        line = jnp.where(lane == step, duty[step], line)
        line = jnp.where(lane == local + step, dwell[step], line)
    packed[...] = line
    landed[me] = line

    @pl.when(me < count - 1)
    def to_later():
        pl.semaphore_wait(barrier, count - 1 - me)

        def send(target, unused):
            push(target).start()
            return 0

        lax.fori_loop(me + 1, count, send, 0)

    diag = (lax.broadcasted_iota(jnp.int32, (LANES, LANES), 0)
            == lax.broadcasted_iota(jnp.int32, (LANES, LANES), 1))
    per = LANES // SUB
    tiles = [slice(LANES * k, LANES * (k + 1)) for k in range(blocks)]
    groups = [slice(SUB * r, SUB * (r + 1)) for r in range(width // SUB)]

    def column(row, k):
        return jnp.sum(jnp.where(diag, row[:, tiles[k]], 0.0), axis=1, keepdims=True)

    for copy in loads[2:]:
        copy.wait()
    decay_row, on_row, off_row = (ref[...].reshape(1, width) for ref in (decay, on, off))
    for level in range(DWELL_MAX + 1):
        keep_row[level] = jnp.broadcast_to(jnp.exp(-float(level) * decay_row), (SUB, width))
    for k in range(blocks):
        rates = column(decay_row, k)
        for level in range(DWELL_MAX + 1):
            keep_col[level, tiles[k]] = jnp.broadcast_to(jnp.exp(-float(level) * rates), (LANES, LANES))
    load.wait()

    totals = [[[None] * blocks for side in range(2)] for source in range(2)]
    for k in range(blocks):
        sources = (column(on_row, k), column(off_row, k))
        for side in range(2):
            for q in range(blocks):
                square = coupling[side, tiles[k], tiles[q]]
                for source in range(2):
                    folded = jnp.sum((square * sources[source]).reshape(per, SUB, LANES), axis=0)
                    old = totals[source][side][q]
                    totals[source][side][q] = folded if old is None else old + folded

    def through(source, side):
        return -jnp.concatenate([jnp.sum(t, axis=0, keepdims=True) for t in totals[source][side]], axis=1)

    through_on = [through(0, side) for side in range(2)]
    through_off = [through(1, side) for side in range(2)]

    def tabulate_duty(level, unused):
        frac = (level.astype(jnp.float32) + 0.5) / DUTY_LEVELS
        for k in range(blocks):
            for q in range(blocks):
                mixing = frac * coupling[0, tiles[k], tiles[q]] + (1.0 - frac) * coupling[1, tiles[k], tiles[q]]
                if k == q:
                    eye = jnp.where(diag, 1.0, 0.0)
                    plus[level, tiles[k], tiles[q]] = eye + mixing
                    turned[level, tiles[k]] = mixing - eye
                else:
                    plus[level, tiles[k], tiles[q]] = mixing
        drive_row[level] = jnp.broadcast_to(frac * on_row + (1.0 - frac) * off_row, (SUB, width))
        mixed_on[level] = jnp.broadcast_to(
            on_row + frac * through_on[0] + (1.0 - frac) * through_on[1], (SUB, width))
        mixed_off[level] = jnp.broadcast_to(
            off_row + frac * through_off[0] + (1.0 - frac) * through_off[1], (SUB, width))
        return 0

    lax.fori_loop(0, DUTY_LEVELS, tabulate_duty, 0)

    def unload(owner):
        return pltpu.make_async_copy(landed.at[owner], codes.at[owner], codes_sem.at[owner])

    def receive(source):
        @pl.when(source < me)
        def arrive():
            pltpu.make_async_remote_copy(
                src_ref=packed, dst_ref=landed.at[source], send_sem=send_sem.at[me], recv_sem=recv_sem.at[source],
                device_id=place_of(source), device_id_type=pl.DeviceIdType.MESH).wait_recv()

    def two_steps(owner, first, state, kept=None):
        duty_a, duty_b = codes[owner, 0, first], codes[owner, 0, first + 1]
        dwell_a, dwell_b = codes[owner, 0, local + first], codes[owner, 0, local + first + 1]
        frac_a = (duty_a.astype(jnp.float32) + 0.5) / DUTY_LEVELS
        scale_a = dwell_a.astype(jnp.float32) / DWELL_MAX
        scale_b = dwell_b.astype(jnp.float32) / DWELL_MAX
        sums = [[None, None] for k in range(blocks)]
        columns = []
        for r, rows in enumerate(groups):
            term = plus[duty_a, rows, tiles[0]] * state[:, tiles[0]]
            for k in range(1, blocks):
                term = term + plus[duty_a, rows, tiles[k]] * state[:, tiles[k]]
            middle = keep_col[dwell_a, rows] * jnp.sum(term, axis=1, keepdims=True)
            if kept is not None:
                columns.append(middle)
            for k in range(blocks):
                if k == r // per:
                    term = turned[duty_b, rows] * middle
                else:
                    term = plus[duty_b, rows, tiles[k]] * middle
                sums[k][r % 2] = term if sums[k][r % 2] is None else sums[k][r % 2] + term
        flat = jnp.concatenate([jnp.sum(s[0] + s[1], axis=0, keepdims=True) for s in sums], axis=1)
        driven = scale_a * (frac_a * mixed_on[duty_b] + (1.0 - frac_a) * mixed_off[duty_b])
        after = keep_row[dwell_b] * (driven - jnp.broadcast_to(flat, (SUB, width)))
        push_b = scale_b * drive_row[duty_b]
        if kept is None:
            return after + push_b
        row = lax.broadcasted_iota(jnp.int32, (local, width), 0)
        flat = jnp.concatenate([
            jnp.sum(jnp.where(diag, jnp.concatenate(columns[per * k:per * (k + 1)], axis=0), 0.0),
                    axis=0, keepdims=True) for k in range(blocks)], axis=1)
        states = jnp.where(row == first, flat, jnp.where(row == first + 1, after[0:1], kept[0]))
        drives = jnp.where(row == first, scale_a * drive_row[duty_a, 0:1],
                           jnp.where(row == first + 1, push_b[0:1], kept[1]))
        return after + push_b, (states, drives)

    half = local // 2
    state = jnp.broadcast_to(x0[...].reshape(1, width), (SUB, width))
    receive(0)
    unload(0).start()

    def block(owner, state):
        receive(owner + 1)
        unload(owner + 1).start()
        unload(owner).wait()
        return lax.fori_loop(0, half, lambda pair, state: two_steps(owner, 2 * pair, state), state)

    state = lax.fori_loop(0, me, block, state)
    unload(me).wait()
    blank = jnp.zeros((local, width), jnp.float32)
    state, kept = lax.fori_loop(
        0, half, lambda pair, carry: two_steps(me, 2 * pair, *carry), (state, (blank, blank)))
    out[...], drive_out[...] = kept

    def finish(target, unused):
        push(target).wait_send()
        return 0

    lax.fori_loop(me + 1, count, finish, 0)


def on_device(initial_state, duty_codes, dwell_counts, coupling, decay_rates, drive_on, drive_off):
    width, local = initial_state.shape[0], duty_codes.shape[0]
    axes = ("outer", "inner")
    count = lax.axis_size(axes[0]) * lax.axis_size(axes[1])
    scratch = [
        pltpu.VMEM((DUTY_LEVELS, width, width), jnp.float32),
        pltpu.VMEM((DUTY_LEVELS, width, LANES), jnp.float32),
        pltpu.VMEM((DWELL_MAX + 1, width, LANES), jnp.float32),
        pltpu.VMEM((DWELL_MAX + 1, SUB, width), jnp.float32),
        pltpu.VMEM((DUTY_LEVELS, SUB, width), jnp.float32),
        pltpu.VMEM((DUTY_LEVELS, SUB, width), jnp.float32),
        pltpu.VMEM((DUTY_LEVELS, SUB, width), jnp.float32),
        pltpu.VMEM(coupling.shape, jnp.float32),
        pltpu.VMEM((1, LANES), jnp.int32),
        pltpu.VMEM((count, 1, LANES), jnp.int32),
        pltpu.SMEM((count, 1, LANES), jnp.int32),
        pltpu.SemaphoreType.DMA((count,)),
        pltpu.SemaphoreType.DMA((count,)),
        pltpu.SemaphoreType.DMA,
        pltpu.SemaphoreType.DMA((count,)),
        pltpu.SMEM((local,), jnp.int32),
        pltpu.SMEM((local,), jnp.int32),
        pltpu.VMEM((width,), jnp.float32),
        pltpu.VMEM((width,), jnp.float32),
        pltpu.VMEM((width,), jnp.float32),
        pltpu.VMEM((width,), jnp.float32),
        pltpu.SemaphoreType.DMA((6,)),
    ]
    vmem = pl.BlockSpec(memory_space=pltpu.VMEM)
    states, drives = pl.pallas_call(
        functools.partial(replay, axes, local),
        out_shape=[jax.ShapeDtypeStruct((local, width), jnp.float32)] * 2,
        in_specs=[pl.BlockSpec(memory_space=pl.ANY)] * 7,
        out_specs=[vmem, vmem],
        scratch_shapes=scratch,
        compiler_params=pltpu.CompilerParams(
            vmem_limit_bytes=56 * 2**20, collective_id=0, has_side_effects=True),
    )(duty_codes, dwell_counts, initial_state, coupling, decay_rates, drive_on, drive_off)
    return states + drives


def solution(mesh):
    return jax.shard_map(
        on_device,
        mesh=mesh,
        in_specs=(
            P("groups"),
            P(("groups", "outer", "inner")),
            P(("groups", "outer", "inner")),
            P(),
            P(),
            P(),
            P(),
        ),
        out_specs=P(("groups", "outer", "inner"), None),
        check_vma=False,
    )
```

```python
import functools
import jax
import jax.numpy as jnp
from jax import lax
from jax.experimental import pallas as pl
from jax.experimental.pallas import tpu as pltpu
from jax.sharding import PartitionSpec as P

DUTY_LEVELS = 16
DWELL_MAX = 8
LANES = 128
SUB = 8


def replay(axes, local, duty_hbm, dwell_hbm, x0_hbm, coupling_hbm, decay_hbm, on_hbm, off_hbm, out,
           plus, turned, keep_col, keep_row, drive_row, mixed_on, mixed_off, coupling, packed, landed,
           codes, send_sem, recv_sem, coupling_sem, codes_sem, duty, dwell, x0, decay, on, off, small_sem):
    width = x0.shape[0]
    blocks = width // LANES
    inner = lax.axis_size(axes[1])
    count = lax.axis_size(axes[0]) * inner
    me = lax.axis_index(axes)

    def place_of(index):
        return {axes[0]: index // inner, axes[1]: index % inner}

    def push(target):
        return pltpu.make_async_remote_copy(
            src_ref=packed, dst_ref=landed.at[me], send_sem=send_sem.at[target], recv_sem=recv_sem.at[me],
            device_id=place_of(target), device_id_type=pl.DeviceIdType.MESH)

    barrier = pltpu.get_barrier_semaphore()

    def greet(source, unused):
        pl.semaphore_signal(barrier, inc=1, device_id=place_of(source), device_id_type=pl.DeviceIdType.MESH)
        return 0

    lax.fori_loop(0, me, greet, 0)
    load = pltpu.make_async_copy(coupling_hbm, coupling, coupling_sem)
    pairs = ((duty_hbm, duty), (dwell_hbm, dwell), (decay_hbm, decay), (on_hbm, on), (off_hbm, off), (x0_hbm, x0))
    loads = [pltpu.make_async_copy(a, b, small_sem.at[i]) for i, (a, b) in enumerate(pairs)]
    for copy in loads:
        copy.start()
    load.start()
    for copy in loads[:2]:
        copy.wait()
    lane = lax.broadcasted_iota(jnp.int32, (1, LANES), 1)
    line = jnp.zeros((1, LANES), jnp.int32)
    for step in range(local):
        line = jnp.where(lane == step, duty[step], line)
        line = jnp.where(lane == local + step, dwell[step], line)
    packed[...] = line
    landed[me] = line

    @pl.when(me < count - 1)
    def to_later():
        pl.semaphore_wait(barrier, count - 1 - me)

        def send(target, unused):
            push(target).start()
            return 0

        lax.fori_loop(me + 1, count, send, 0)

    diag = (lax.broadcasted_iota(jnp.int32, (LANES, LANES), 0)
            == lax.broadcasted_iota(jnp.int32, (LANES, LANES), 1))
    per = LANES // SUB
    tiles = [slice(LANES * k, LANES * (k + 1)) for k in range(blocks)]
    groups = [slice(SUB * r, SUB * (r + 1)) for r in range(width // SUB)]

    def column(row, k):
        return jnp.sum(jnp.where(diag, row[:, tiles[k]], 0.0), axis=1, keepdims=True)

    for copy in loads[2:]:
        copy.wait()
    decay_row, on_row, off_row = (ref[...].reshape(1, width) for ref in (decay, on, off))
    for level in range(DWELL_MAX + 1):
        keep_row[level] = jnp.broadcast_to(jnp.exp(-float(level) * decay_row), (SUB, width))
    for k in range(blocks):
        rates = column(decay_row, k)
        for level in range(DWELL_MAX + 1):
            keep_col[level, tiles[k]] = jnp.broadcast_to(jnp.exp(-float(level) * rates), (LANES, LANES))
    load.wait()

    totals = [[[None] * blocks for side in range(2)] for source in range(2)]
    for k in range(blocks):
        sources = (column(on_row, k), column(off_row, k))
        for side in range(2):
            for q in range(blocks):
                square = coupling[side, tiles[k], tiles[q]]
                for source in range(2):
                    folded = jnp.sum((square * sources[source]).reshape(per, SUB, LANES), axis=0)
                    old = totals[source][side][q]
                    totals[source][side][q] = folded if old is None else old + folded

    def through(source, side):
        return -jnp.concatenate([jnp.sum(t, axis=0, keepdims=True) for t in totals[source][side]], axis=1)

    through_on = [through(0, side) for side in range(2)]
    through_off = [through(1, side) for side in range(2)]

    def tabulate_duty(level, unused):
        frac = (level.astype(jnp.float32) + 0.5) / DUTY_LEVELS
        for k in range(blocks):
            for q in range(blocks):
                mixing = frac * coupling[0, tiles[k], tiles[q]] + (1.0 - frac) * coupling[1, tiles[k], tiles[q]]
                if k == q:
                    eye = jnp.where(diag, 1.0, 0.0)
                    plus[level, tiles[k], tiles[q]] = eye + mixing
                    turned[level, tiles[k]] = mixing - eye
                else:
                    plus[level, tiles[k], tiles[q]] = mixing
        drive_row[level] = jnp.broadcast_to(frac * on_row + (1.0 - frac) * off_row, (SUB, width))
        mixed_on[level] = jnp.broadcast_to(
            on_row + frac * through_on[0] + (1.0 - frac) * through_on[1], (SUB, width))
        mixed_off[level] = jnp.broadcast_to(
            off_row + frac * through_off[0] + (1.0 - frac) * through_off[1], (SUB, width))
        return 0

    lax.fori_loop(0, DUTY_LEVELS, tabulate_duty, 0)

    def unload(owner):
        return pltpu.make_async_copy(landed.at[owner], codes.at[owner], codes_sem.at[owner])

    def receive(source):
        @pl.when(source < me)
        def arrive():
            pltpu.make_async_remote_copy(
                src_ref=packed, dst_ref=landed.at[source], send_sem=send_sem.at[me], recv_sem=recv_sem.at[source],
                device_id=place_of(source), device_id_type=pl.DeviceIdType.MESH).wait_recv()

    def two_steps(owner, first, state, kept=None):
        duty_a, duty_b = codes[owner, 0, first], codes[owner, 0, first + 1]
        dwell_a, dwell_b = codes[owner, 0, local + first], codes[owner, 0, local + first + 1]
        frac_a = (duty_a.astype(jnp.float32) + 0.5) / DUTY_LEVELS
        scale_a = dwell_a.astype(jnp.float32) / DWELL_MAX
        scale_b = dwell_b.astype(jnp.float32) / DWELL_MAX
        sums = [[None, None] for k in range(blocks)]
        columns = []
        for r, rows in enumerate(groups):
            term = plus[duty_a, rows, tiles[0]] * state[:, tiles[0]]
            for k in range(1, blocks):
                term = term + plus[duty_a, rows, tiles[k]] * state[:, tiles[k]]
            middle = keep_col[dwell_a, rows] * jnp.sum(term, axis=1, keepdims=True)
            if kept is not None:
                columns.append(middle)
            for k in range(blocks):
                if k == r // per:
                    term = turned[duty_b, rows] * middle
                else:
                    term = plus[duty_b, rows, tiles[k]] * middle
                sums[k][r % 2] = term if sums[k][r % 2] is None else sums[k][r % 2] + term
        flat = jnp.concatenate([jnp.sum(s[0] + s[1], axis=0, keepdims=True) for s in sums], axis=1)
        driven = scale_a * (frac_a * mixed_on[duty_b] + (1.0 - frac_a) * mixed_off[duty_b])
        after = keep_row[dwell_b] * (driven - jnp.broadcast_to(flat, (SUB, width)))
        push_b = scale_b * drive_row[duty_b]
        if kept is None:
            return after + push_b
        row = lax.broadcasted_iota(jnp.int32, (local, width), 0)
        flat = jnp.concatenate([
            jnp.sum(jnp.where(diag, jnp.concatenate(columns[per * k:per * (k + 1)], axis=0), 0.0),
                    axis=0, keepdims=True) for k in range(blocks)], axis=1)
        after = after + push_b
        flat = flat + scale_a * drive_row[duty_a, 0:1]
        return after, jnp.where(row == first, flat, jnp.where(row == first + 1, after[0:1], kept))

    half = local // 2
    state = jnp.broadcast_to(x0[...].reshape(1, width), (SUB, width))
    receive(0)
    unload(0).start()

    def block(owner, state):
        receive(owner + 1)
        unload(owner + 1).start()
        unload(owner).wait()
        return lax.fori_loop(0, half, lambda pair, state: two_steps(owner, 2 * pair, state), state)

    state = lax.fori_loop(0, me, block, state)
    unload(me).wait()
    blank = jnp.zeros((local, width), jnp.float32)
    state, kept = lax.fori_loop(
        0, half, lambda pair, carry: two_steps(me, 2 * pair, *carry), (state, blank))
    out[...] = kept

    def finish(target, unused):
        push(target).wait_send()
        return 0

    lax.fori_loop(me + 1, count, finish, 0)


def on_device(initial_state, duty_codes, dwell_counts, coupling, decay_rates, drive_on, drive_off):
    width, local = initial_state.shape[0], duty_codes.shape[0]
    axes = ("outer", "inner")
    count = lax.axis_size(axes[0]) * lax.axis_size(axes[1])
    scratch = [
        pltpu.VMEM((DUTY_LEVELS, width, width), jnp.float32),
        pltpu.VMEM((DUTY_LEVELS, width, LANES), jnp.float32),
        pltpu.VMEM((DWELL_MAX + 1, width, LANES), jnp.float32),
        pltpu.VMEM((DWELL_MAX + 1, SUB, width), jnp.float32),
        pltpu.VMEM((DUTY_LEVELS, SUB, width), jnp.float32),
        pltpu.VMEM((DUTY_LEVELS, SUB, width), jnp.float32),
        pltpu.VMEM((DUTY_LEVELS, SUB, width), jnp.float32),
        pltpu.VMEM(coupling.shape, jnp.float32),
        pltpu.VMEM((1, LANES), jnp.int32),
        pltpu.VMEM((count, 1, LANES), jnp.int32),
        pltpu.SMEM((count, 1, LANES), jnp.int32),
        pltpu.SemaphoreType.DMA((count,)),
        pltpu.SemaphoreType.DMA((count,)),
        pltpu.SemaphoreType.DMA,
        pltpu.SemaphoreType.DMA((count,)),
        pltpu.SMEM((local,), jnp.int32),
        pltpu.SMEM((local,), jnp.int32),
        pltpu.VMEM((width,), jnp.float32),
        pltpu.VMEM((width,), jnp.float32),
        pltpu.VMEM((width,), jnp.float32),
        pltpu.VMEM((width,), jnp.float32),
        pltpu.SemaphoreType.DMA((6,)),
    ]
    vmem = pl.BlockSpec(memory_space=pltpu.VMEM)
    return pl.pallas_call(
        functools.partial(replay, axes, local),
        out_shape=jax.ShapeDtypeStruct((local, width), jnp.float32),
        in_specs=[pl.BlockSpec(memory_space=pl.ANY)] * 7,
        out_specs=vmem,
        scratch_shapes=scratch,
        compiler_params=pltpu.CompilerParams(
            vmem_limit_bytes=56 * 2**20, collective_id=0, has_side_effects=True),
    )(duty_codes, dwell_counts, initial_state, coupling, decay_rates, drive_on, drive_off)


def solution(mesh):
    return jax.shard_map(
        on_device,
        mesh=mesh,
        in_specs=(
            P("groups"),
            P(("groups", "outer", "inner")),
            P(("groups", "outer", "inner")),
            P(),
            P(),
            P(),
            P(),
        ),
        out_specs=P(("groups", "outer", "inner"), None),
        check_vma=False,
    )
```
